512 devices in a mesh: rep: 32 (over x, y_hi, core), chan: 16 (over y_lo, z).
Axes of the slice: x: 4, y: 8 (y_hi: 4, y_lo: 2; y = y_hi * 2 + y_lo), z: 8, core: 2. Of those that a mesh axis runs over, the one named last changes fastest.
Arguments:
- features: bfloat16 [32, 512, 1024], P('rep', 'chan'), may hold values from -6 to 6
- filters: bfloat16 [9, 512, 512], P(None, 'chan'), may hold values from -0.09375 to 0.09375
- cotangent: bfloat16 [32, 512, 1024], P('rep', 'chan'), may hold values from -6 to 6
Outputs:
- result_maps: bfloat16 [32, 512, 1024], P('rep', 'chan')
- input_grad: bfloat16 [32, 512, 1024], P('rep', 'chan')
- filter_grad: float32 [9, 512, 512], P(None, 'chan')
The draws below stay inside these ranges and needn't reach their ends.
All inputs are finite; a program needn't handle non-finite values.
Results may differ from the reference program's by a relative error of at most 0.001.
Values may be sent and summed in bfloat16 or wider, within the bound.
A program may use at most 64 MiB of HBM per device.

```python
import jax
import jax.numpy as jnp
from jax import lax

CH = 512
MAP_W = 64
CELLS = 1024
SAMPLES = 32


def steps_of(key, dims, cuts, smallest, high):
    gain = 1.0
    for position, blocks in cuts:
        steps = jax.random.uniform(jax.random.fold_in(jax.random.fold_in(key, 6), position), (blocks,), jnp.float32, smallest / len(cuts), high / len(cuts))
        gain = gain * jnp.repeat(jnp.exp(steps), dims[position] // blocks).reshape((-1,) + (1,) * (len(dims) - 1 - position))
    return gain


def noise(stream_key, extent, width, most, cuts=(), dtype=jnp.bfloat16):
    entries = jax.random.normal(stream_key, extent, jnp.float32) * width
    if len(cuts) > 0:
        entries = steps_of(stream_key, extent, cuts, -0.22, 0.18) * entries
    return jnp.clip(entries, min=-most, max=most).astype(dtype)


def setup_inputs(seed: int = 0) -> dict:
    streams_of = jax.random.split(jax.random.key(seed), 4)
    features = noise(streams_of[0], (SAMPLES, CH, CELLS), 1.0, 6.0, ((0, 32), (1, 16)))
    filters = noise(streams_of[1], (9, CH, CH), (9 * CH) ** -0.5, 0.09375, ((1, 16),))
    cotangent = noise(streams_of[2], (SAMPLES, CH, CELLS), 1.0, 6.0, ((0, 32), (1, 16)))
    return {"features": features, "filters": filters, "cotangent": cotangent}


offsets = [(a, b) for a in (-1, 0, 1) for b in (-1, 0, 1)]


def shifted(value, row_step, col_step):
    cells = value.shape[-1]
    margin = MAP_W + 1
    padded = jnp.pad(value, [(0, 0)] * (value.ndim - 1) + [(margin, margin)])
    begin = margin + row_step * MAP_W + col_step
    taken = lax.slice_in_dim(padded, begin, begin + cells, axis=value.ndim - 1)
    column = jnp.arange(cells) % MAP_W + col_step
    keep = (column >= 0) & (column < MAP_W)
    return jnp.where(keep, taken, jnp.zeros_like(taken))


def reference(features, filters, cotangent):
    def forward_one(feat):
        total = jnp.zeros((CH, CELLS), jnp.float32)
        for index, (row_step, col_step) in enumerate(offsets):
            total = total + jnp.dot(filters[index].T, shifted(feat, row_step, col_step), preferred_element_type=jnp.float32)
        return total.astype(jnp.bfloat16)

    def backward_one(grad):
        total = jnp.zeros((CH, CELLS), jnp.float32)
        for index, (row_step, col_step) in enumerate(offsets):
            total = total + jnp.dot(filters[index], shifted(grad, -row_step, -col_step), preferred_element_type=jnp.float32)
        return total.astype(jnp.bfloat16)

    def accumulate(carry, pair):
        feat, grad = pair
        terms = []
        for index, (row_step, col_step) in enumerate(offsets):
            terms.append(jnp.dot(shifted(feat, row_step, col_step), grad.T, preferred_element_type=jnp.float32))
        return carry + jnp.stack(terms), None

    result_maps = lax.map(forward_one, features)
    input_grad = lax.map(backward_one, cotangent)
    summed, unused = lax.scan(accumulate, jnp.zeros((9, CH, CH), jnp.float32), (features, cotangent))
    filter_grad = summed / SAMPLES
    return (result_maps, input_grad, filter_grad)
```

```python
import jax
import jax.numpy as jnp
from jax import lax
from jax.experimental import pallas as pl
from jax.experimental.pallas import tpu as pltpu
from jax.sharding import PartitionSpec as P

MESH = pl.DeviceIdType.MESH
F32 = jnp.float32
BF16 = jnp.bfloat16

CELLS = 1024
OFFSETS = [(a, b) for a in (-1, 0, 1) for b in (-1, 0, 1)]

STEPS = [
    [(0, 0, 0, 1, 0), (0, 0, 0, -1, 0), (0, 0, 1, 0, 0), (0, 0, 0, 2, 0), (0, 0, 0, -2, 0)],
    [(0, -1, 1, 0, 0), (0, 1, 1, 0, 0), (0, -2, 0, 1, 0), (0, 2, 0, -1, 0), (0, -2, 1, 0, 0), (0, 2, 1, 0, 0),
     (0, -2, 0, 2, 1), (0, 2, 0, -2, 2)],
    [(1, -2, 0, 1, 0), (1, 2, 0, -1, 0), (1, -2, 0, 2, 1), (1, 2, 0, -2, 2)],
]
COPIES = sum(len(s) for s in STEPS)
CHIPS = [(dx, dh) for dx in range(4) for dh in range(4) if (dx, dh) != (0, 0)]
PEERS = [(dy, dz) for dy in range(2) for dz in range(8) if (dy, dz) != (0, 0)]


def coords():
    rep = lax.axis_index("rep")
    chan = lax.axis_index("chan")
    return rep // 8, (rep // 2) % 4, rep % 2, chan // 8, chan % 8


def keep_mask(a, b):
    p = lax.broadcasted_iota(jnp.int32, (32, CELLS), 1)
    row = p // 64 + a
    col = p % 64 + b
    return (row >= 0) & (row < 16) & (col >= 0) & (col < 64)


def moved(value, a, b):
    step = 64 * a + b
    if step == 0:
        return value
    return jnp.where(keep_mask(a, b), pltpu.roll(value, (-step) % CELLS, 1), 0.0)


def kernel(feat, filt, cot, maps_out, igrad_out, fgrad_out,
           c_all, f_all, w_all, w_send, taps, prod, grad, pair, half, slots, mine, full,
           c_ss, c_rs, f_ss, f_rs, w_ss, w_rs, r_ss, r_rs, a_ss, a_rs, k_ss, k_rs):
    x, h, core, yl, z = coords()
    rep = lax.axis_index("rep")
    chan = lax.axis_index("chan")

    def chan_dev(dy, dz):
        return (rep, ((yl + dy) % 2) * 8 + (z + dz + 8) % 8)

    def chip_dev(dx, dh):
        return ((((x + dx) % 4) * 4 + (h + dh) % 4) * 2 + core, chan)

    sibling = ((x * 4 + h) * 2 + 1 - core, chan)

    barrier = pltpu.get_barrier_semaphore()
    for dev in [chan_dev(*d) for d in PEERS] + [chip_dev(*d) for d in CHIPS] + [sibling]:
        pl.semaphore_signal(barrier, inc=1, device_id=dev, device_id_type=MESH)

    own_rows = pl.ds(pl.multiple_of(chan * 32, 32), 32)
    c_all[own_rows, :] = cot[0]
    f_all[own_rows, :] = feat[0]
    pl.semaphore_wait(barrier, len(PEERS) + len(CHIPS) + 1)

    def cols(part):
        return [pl.ds(0, CELLS), pl.ds(0, CELLS // 2), pl.ds(CELLS // 2, CELLS // 2)][part]

    def gather(own, buf, ss, rs):
        def rows(dy, dz):
            owner = ((yl + dy) % 2) * 8 + (z + dz + 8) % 8
            return pl.ds(pl.multiple_of(owner * 32, 32), 32)

        def send_copy(n, item):
            dy, dz, hy, hz, part = item
            src = own.at[0, :, cols(part)] if (dy, dz) == (0, 0) else buf.at[rows(dy, dz), cols(part)]
            return pltpu.make_async_remote_copy(
                src_ref=src, dst_ref=buf.at[rows(dy, dz), cols(part)],
                send_sem=ss.at[n], recv_sem=rs.at[n],
                device_id=chan_dev(hy, hz), device_id_type=MESH)

        def recv_copy(n, item):
            dy, dz, hy, hz, part = item
            place = buf.at[rows(dy + hy, dz - hz), cols(part)]
            return pltpu.make_async_remote_copy(
                src_ref=place, dst_ref=place,
                send_sem=ss.at[n], recv_sem=rs.at[n],
                device_id=chan_dev(hy, hz), device_id_type=MESH)

        numbered, n = [], 0
        for step in STEPS:
            numbered.append([(n + k, item) for k, item in enumerate(step)])
            n += len(step)

        def send(s):
            for n, item in numbered[s]:
                send_copy(n, item).start()

        def recv(s):
            for n, item in numbered[s]:
                recv_copy(n, item).wait_recv()

        def drain():
            for step in numbered:
                for n, item in step:
                    send_copy(n, item).wait_send()

        return send, recv, drain

    c_send, c_recv, c_drain = gather(cot, c_all, c_ss, c_rs)
    f_send, f_recv, f_drain = gather(feat, f_all, f_ss, f_rs)

    c_send(0)

    value = feat[0].astype(F32)
    for t, (a, b) in enumerate(OFFSETS):
        taps[t * 32:(t + 1) * 32, :] = moved(value, a, b).astype(BF16)
    grad[9] = jnp.zeros((32, 512), F32)

    c_recv(0)
    c_send(1)

    for d in range(16):
        parts = [filt[t, :, d * 32:(d + 1) * 32].astype(F32) for t in range(9)]
        parts.append(jnp.zeros((32, 96), F32))
        w_send[d] = jnp.concatenate(parts, axis=1).astype(BF16)
    my_rows = pl.ds(pl.multiple_of(core * 16, 16), 16)
    their_rows = pl.ds(pl.multiple_of((1 - core) * 16, 16), 16)
    w_all[chan] = w_send[chan]

    c_recv(1)
    c_send(2)
    f_send(0)

    def w_copy(n, dy, dz):
        to = ((yl + dy) % 2) * 8 + (z + dz) % 8
        return pltpu.make_async_remote_copy(
            src_ref=w_send.at[to, my_rows], dst_ref=w_all.at[chan, my_rows],
            send_sem=w_ss.at[n], recv_sem=w_rs.at[n],
            device_id=chan_dev(dy, dz), device_id_type=MESH)

    def w_arrival(n, dy, dz):
        place = w_all.at[((yl + dy) % 2) * 8 + (z - dz + 8) % 8, my_rows]
        return pltpu.make_async_remote_copy(
            src_ref=place, dst_ref=place, send_sem=w_ss.at[n], recv_sem=w_rs.at[n],
            device_id=chan_dev(dy, dz), device_id_type=MESH)

    for n, (dy, dz) in enumerate(PEERS):
        w_copy(n, dy, dz).start()

    c_recv(2)

    def grad_tile(n, _):
        rows = pl.ds(pl.multiple_of(n * 256, 256), 256)
        tile = lax.dot_general(taps[...], c_all[rows, :], (((1,), (1,)), ((), ())), preferred_element_type=F32)
        grad[0:9, :, rows] = tile.reshape(9, 32, 256)
        return 0

    lax.fori_loop(0, 2, grad_tile, 0)

    def sib_copy(n, src, dst):
        return pltpu.make_async_remote_copy(
            src_ref=src, dst_ref=dst, send_sem=k_ss.at[n], recv_sem=k_rs.at[n],
            device_id=sibling, device_id_type=MESH)

    my_taps = pl.ds(core * 5, 5)
    other_taps = pl.ds((1 - core) * 5, 5)
    pair_copy = sib_copy(0, grad.at[other_taps], pair)
    pair_copy.start()

    f_recv(0)
    f_send(1)

    pair_copy.wait()
    half[...] = grad[my_taps] + pair[...]

    def place(dx, dh):
        return pl.ds(pl.multiple_of(((h + dh) % 4) * 8, 8), 8), pl.ds(pl.multiple_of(((x + dx) % 4) * 128, 128), 128)

    def rs_copy(n, dx, dh):
        r, c = place(dx, dh)
        return pltpu.make_async_remote_copy(
            src_ref=half.at[:, r, c], dst_ref=slots.at[n],
            send_sem=r_ss.at[n], recv_sem=r_rs.at[n],
            device_id=chip_dev(dx, dh), device_id_type=MESH)

    for n, d in enumerate(CHIPS):
        rs_copy(n, *d).start()

    def tap_products(lhs, rhs):
        def tile(n, _):
            c = pl.ds(pl.multiple_of(n * 256, 256), 256)
            prod[:, c] = lhs(rhs[:, c])
            return 0

        lax.fori_loop(0, 4, tile, 0)

    def tap_sum(sign):
        total = prod[4 * 32:5 * 32, :]
        for t, (a, b) in enumerate(OFFSETS):
            if t != 4:
                total = total + moved(prod[t * 32:(t + 1) * 32, :], sign * a, sign * b)
        return total

    tap_products(lambda v: jnp.dot(filt[...].reshape(288, 512), v, preferred_element_type=F32), c_all)
    igrad_out[0] = tap_sum(-1).astype(BF16)

    f_recv(1)
    f_send(2)

    r0, c0 = place(0, 0)
    for n, d in enumerate(CHIPS):
        rs_copy(n, *d).wait_recv()
    total = half[:, r0, c0]
    for n in range(15):
        total = total + slots[n]
    total = total * (1.0 / 32.0)
    mine[...] = total
    full[my_taps, r0, c0] = total

    def ag_copy(n, dx, dh):
        return pltpu.make_async_remote_copy(
            src_ref=mine, dst_ref=full.at[my_taps, r0, c0],
            send_sem=a_ss.at[n], recv_sem=a_rs.at[n],
            device_id=chip_dev(dx, dh), device_id_type=MESH)

    def ag_arrival(n, dx, dh):
        r, c = place(4 - dx, 4 - dh)
        spot = full.at[my_taps, r, c]
        return pltpu.make_async_remote_copy(
            src_ref=spot, dst_ref=spot, send_sem=a_ss.at[n], recv_sem=a_rs.at[n],
            device_id=chip_dev(dx, dh), device_id_type=MESH)

    for n, d in enumerate(CHIPS):
        ag_copy(n, *d).start()

    for n, d in enumerate(PEERS):
        w_arrival(n, *d).wait_recv()
    w_pair = sib_copy(1, w_all.at[:, my_rows], w_all.at[:, my_rows])
    w_pair_in = sib_copy(1, w_all.at[:, their_rows], w_all.at[:, their_rows])
    w_pair.start()
    f_recv(2)
    w_pair_in.wait_recv()

    def forward(v):
        return lax.dot_general(w_all[...].reshape(512, 384)[:, :288], v, (((0,), (0,)), ((), ())),
                               preferred_element_type=F32)

    tap_products(forward, f_all)
    maps_out[0] = tap_sum(1).astype(BF16)

    for n, d in enumerate(CHIPS):
        ag_arrival(n, *d).wait_recv()
    out_pair = sib_copy(2, full.at[my_taps], full.at[my_taps])
    out_pair_in = sib_copy(2, full.at[other_taps], full.at[other_taps])
    out_pair.start()
    out_pair_in.wait_recv()
    fgrad_out[...] = full[0:9]

    out_pair.wait_send()
    w_pair.wait_send()
    c_drain()
    f_drain()
    for n, d in enumerate(PEERS):
        w_copy(n, *d).wait_send()
    for n, d in enumerate(CHIPS):
        rs_copy(n, *d).wait_send()
        ag_copy(n, *d).wait_send()


def per_device(features, filters, cotangent):
    vmem = pl.BlockSpec(memory_space=pltpu.VMEM)
    dma = pltpu.SemaphoreType.DMA
    return tuple(pl.pallas_call(
        kernel,
        out_shape=(
            jax.ShapeDtypeStruct((1, 32, CELLS), BF16),
            jax.ShapeDtypeStruct((1, 32, CELLS), BF16),
            jax.ShapeDtypeStruct((9, 32, 512), F32),
        ),
        in_specs=[vmem] * 3,
        out_specs=(vmem,) * 3,
        scratch_shapes=[
            pltpu.VMEM((512, CELLS), BF16),
            pltpu.VMEM((512, CELLS), BF16),
            pltpu.VMEM((16, 32, 384), BF16),
            pltpu.VMEM((16, 32, 384), BF16),
            pltpu.VMEM((288, CELLS), BF16),
            pltpu.VMEM((288, CELLS), F32),
            pltpu.VMEM((10, 32, 512), F32),
            pltpu.VMEM((5, 32, 512), F32),
            pltpu.VMEM((5, 32, 512), F32),
            pltpu.VMEM((15, 5, 8, 128), F32),
            pltpu.VMEM((5, 8, 128), F32),
            pltpu.VMEM((10, 32, 512), F32),
            dma((COPIES,)), dma((COPIES,)), dma((COPIES,)), dma((COPIES,)),
            dma((15,)), dma((15,)), dma((15,)), dma((15,)), dma((15,)), dma((15,)),
            dma((3,)), dma((3,)),
        ],
        compiler_params=pltpu.CompilerParams(
            collective_id=0, has_side_effects=True, vmem_limit_bytes=32 * 1024 * 1024),
        cost_estimate=pl.CostEstimate(flops=906_000_000, bytes_accessed=1_200_000, transcendentals=0),
        name="conv",
    )(features, filters, cotangent))


def solution(mesh):
    return jax.shard_map(
        per_device,
        mesh=mesh,
        in_specs=(P("rep", "chan", None), P(None, "chan", None), P("rep", "chan", None)),
        out_specs=(P("rep", "chan", None), P("rep", "chan", None), P(None, "chan", None)),
        check_vma=False,
    )
```

```python
import jax
import jax.numpy as jnp
from jax import lax
from jax.experimental import pallas as pl
from jax.experimental.pallas import tpu as pltpu
from jax.sharding import PartitionSpec as P

MESH = pl.DeviceIdType.MESH
F32 = jnp.float32
BF16 = jnp.bfloat16

CELLS = 1024
OFFSETS = [(a, b) for a in (-1, 0, 1) for b in (-1, 0, 1)]
CHIPS = [(dx, dh) for dx in range(4) for dh in range(4) if (dx, dh) != (0, 0)]
PEERS = [(dy, dz) for dy in range(2) for dz in range(8) if (dy, dz) != (0, 0)]
NSEM = 96


def coords():
    rep = lax.axis_index("rep")
    chan = lax.axis_index("chan")
    return rep // 8, (rep // 2) % 4, rep % 2, chan // 8, chan % 8


def keep_mask(a, b):
    p = lax.broadcasted_iota(jnp.int32, (32, CELLS), 1)
    row = p // 64 + a
    col = p % 64 + b
    return (row >= 0) & (row < 16) & (col >= 0) & (col < 64)


def moved(value, a, b):
    step = 64 * a + b
    if step == 0:
        return value
    return jnp.where(keep_mask(a, b), pltpu.roll(value, (-step) % CELLS, 1), 0.0)


def kernel(feat_in, filt_in, cot_in, maps_out, igrad_out, fgrad_out,
           filt, c_all, f_all, w_all, w_send, taps, prod, grad, pair, half, slots, mine, full,
           in_sem, ss, rs, r_ss, r_rs):
    x, h, core, yl, z = coords()
    rep = lax.axis_index("rep")
    chan = lax.axis_index("chan")

    def chan_of(dy, dz):
        return ((yl + dy) % 2) * 8 + (z + dz + 8) % 8

    def chan_dev(dy, dz):
        return (rep, chan_of(dy, dz))

    def chip_dev(dx, dh):
        return ((((x + dx) % 4) * 4 + (h + dh) % 4) * 2 + core, chan)

    sibling = ((x * 4 + h) * 2 + 1 - core, chan)

    def rows(dy, dz):
        return pl.ds(pl.multiple_of(chan_of(dy, dz) * 32, 32), 32)

    barrier = pltpu.get_barrier_semaphore()
    for dev in [chan_dev(*d) for d in PEERS] + [chip_dev(*d) for d in CHIPS] + [sibling]:
        pl.semaphore_signal(barrier, inc=1, device_id=dev, device_id_type=MESH)

    loads = [
        pltpu.make_async_copy(cot_in.at[0], c_all.at[rows(0, 0)], in_sem.at[0]),
        pltpu.make_async_copy(feat_in.at[0], f_all.at[rows(0, 0)], in_sem.at[1]),
        pltpu.make_async_copy(filt_in, filt, in_sem.at[2]),
    ]
    for load in loads:
        load.start()
    for load in loads:
        load.wait()
    pl.semaphore_wait(barrier, len(PEERS) + len(CHIPS) + 1)

    sends, pending = [], {}

    def start(key, src, dst, arrival, dev):
        n = len(sends)
        copy = pltpu.make_async_remote_copy(
            src_ref=src, dst_ref=dst, send_sem=ss.at[n], recv_sem=rs.at[n], device_id=dev, device_id_type=MESH)
        copy.start()
        sends.append(copy)
        pending[key] = pltpu.make_async_remote_copy(
            src_ref=arrival, dst_ref=arrival, send_sem=ss.at[n], recv_sem=rs.at[n], device_id=dev, device_id_type=MESH)

    def arrive(key):
        pending.pop(key).wait_recv()

    def pass_on(name, buf, dy, dz, hy, hz, part=0):
        cols = [pl.ds(0, CELLS), pl.ds(0, CELLS // 2), pl.ds(CELLS // 2, CELLS // 2)][part]
        place = buf.at[rows(dy, dz), cols]
        start((name, (dy + hy) % 2, dz - hz, part), place, place, buf.at[rows(dy + hy, dz - hz), cols], chan_dev(hy, hz))

    pass_on("c", c_all, 0, 0, 1, 0)
    for dz in (1, -1, 2, -2, 3, -3):
        pass_on("c", c_all, 0, 0, 0, dz)
    pass_on("f", f_all, 0, 0, 1, 0)

    value = f_all[rows(0, 0), :].astype(F32)
    for t, (a, b) in enumerate(OFFSETS):
        taps[t * 32:(t + 1) * 32, :] = moved(value, a, b).astype(BF16)
    grad[9] = jnp.zeros((32, 512), F32)

    for dz in (1, -1, 2, -2):
        arrive(("c", 0, dz, 0))
        pass_on("c", c_all, 0, dz, 1, 0)
    for dz in (3, -3):
        arrive(("c", 0, dz, 0))
        if dz == 3:
            pass_on("c", c_all, 0, 3, 0, -1, 1)
        else:
            pass_on("c", c_all, 0, -3, 0, 1, 2)
        pass_on("c", c_all, 0, dz, 1, 0)

    arrive(("f", 1, 0, 0))
    for dz in (1, -1, 2, -2, 3, -3):
        for dy in (0, 1):
            pass_on("f", f_all, dy, 0, 0, dz)

    for d in range(16):
        parts = [filt[t, :, d * 32:(d + 1) * 32].astype(F32) for t in range(9)]
        parts.append(jnp.zeros((32, 96), F32))
        w_send[d] = jnp.concatenate(parts, axis=1).astype(BF16)
    my_rows = pl.ds(pl.multiple_of(core * 16, 16), 16)
    their_rows = pl.ds(pl.multiple_of((1 - core) * 16, 16), 16)
    w_all[chan] = w_send[chan]

    arrive(("c", 0, 4, 1))
    pass_on("c", c_all, 0, 4, 1, 0, 1)
    arrive(("c", 0, -4, 2))
    pass_on("c", c_all, 0, -4, 1, 0, 2)

    my_taps = pl.ds(core * 5, 5)
    other_taps = pl.ds((1 - core) * 5, 5)

    def place(lane_tile, dh):
        return pl.ds(pl.multiple_of(((h + dh) % 4) * 8, 8), 8), pl.ds(pl.multiple_of(lane_tile * 128, 128), 128)

    def column(dy):
        return pl.ds(pl.multiple_of(((yl + dy) % 2) * 256, 256), 256)

    def grad_column(dy):
        side = column(dy)
        tile = lax.dot_general(taps[...], c_all[side, :], (((1,), (1,)), ((), ())), preferred_element_type=F32)
        grad[0:9, :, side] = tile.reshape(9, 32, 256)
        start(("pair", dy), grad.at[other_taps, :, side], pair.at[:, :, side], pair.at[:, :, side], sibling)

    def reduce_copy(n, lane_tile, dh):
        r, c = place(lane_tile, dh)
        return pltpu.make_async_remote_copy(
            src_ref=half.at[:, r, c], dst_ref=slots.at[n], send_sem=r_ss.at[n], recv_sem=r_rs.at[n],
            device_id=((lane_tile * 4 + (h + dh) % 4) * 2 + core, chan), device_id_type=MESH)

    def reduce_column(dy):
        side = column(dy)
        arrive(("pair", dy))
        half[:, :, side] = grad[my_taps, :, side] + pair[:, :, side]
        for k in (0, 1):
            lane_tile = ((yl + dy) % 2) * 2 + k
            for dh in range(4):
                n = ((lane_tile - x + 4) % 4) * 4 + dh

                @pl.when(n != 0)
                def _():
                    reduce_copy(n, lane_tile, dh).start()

    grad_column(0)
    reduce_column(0)

    for n, (dy, dz) in enumerate(PEERS):
        start(("w", n), w_send.at[chan_of(dy, dz), my_rows], w_all.at[chan, my_rows],
              w_all.at[chan_of(dy, -dz), my_rows], chan_dev(dy, dz))

    for dz in (0, 1, -1, 2, -2, 3, -3):
        arrive(("c", 1, dz, 0))
    arrive(("c", 1, 4, 1))
    arrive(("c", 1, -4, 2))
    grad_column(1)
    reduce_column(1)

    def tap_products(lhs, rhs):
        def tile(n, _):
            c = pl.ds(pl.multiple_of(n * 256, 256), 256)
            prod[:, c] = lhs(rhs[:, c])
            return 0

        lax.fori_loop(0, 4, tile, 0)

    def tap_sum(sign):
        total = prod[4 * 32:5 * 32, :]
        for t, (a, b) in enumerate(OFFSETS):
            if t != 4:
                total = total + moved(prod[t * 32:(t + 1) * 32, :], sign * a, sign * b)
        return total

    tap_products(lambda v: jnp.dot(filt[...].reshape(288, 512), v, preferred_element_type=F32), c_all)
    igrad_out[0] = tap_sum(-1).astype(BF16)

    r0, c0 = place(x, 0)
    for n in range(1, 16):
        reduce_copy(n, x, 0).wait_recv()
    total = half[:, r0, c0]
    for n in range(1, 16):
        total = total + slots[n]
    total = total * (1.0 / 32.0)
    mine[...] = total
    full[my_taps, r0, c0] = total
    for dx, dh in CHIPS:
        r, c = place((x + 4 - dx) % 4, 4 - dh)
        start(("a", dx, dh), mine, full.at[my_taps, r0, c0], full.at[my_taps, r, c], chip_dev(dx, dh))

    def to_sibling(dx, dh):
        r, c = place((x + 4 - dx) % 4, 4 - dh)
        start(("o", dx, dh), full.at[my_taps, r, c], full.at[my_taps, r, c], full.at[other_taps, r, c], sibling)

    to_sibling(0, 0)

    for dy in (0, 1):
        arrive(("f", dy, 3, 0))
        pass_on("f", f_all, dy, 3, 0, -1, 1)
        arrive(("f", dy, -3, 0))
        pass_on("f", f_all, dy, -3, 0, 1, 2)

    for n, d in enumerate(PEERS):
        arrive(("w", n))
    start("wpair", w_all.at[:, my_rows], w_all.at[:, my_rows], w_all.at[:, their_rows], sibling)
    for dy in (0, 1):
        for dz in (1, -1, 2, -2):
            arrive(("f", dy, dz, 0))
        arrive(("f", dy, 4, 1))
        arrive(("f", dy, -4, 2))
    arrive("wpair")

    def forward(v):
        return lax.dot_general(w_all[...].reshape(512, 384)[:, :288], v, (((0,), (0,)), ((), ())),
                               preferred_element_type=F32)

    tap_products(forward, f_all)
    maps_out[0] = tap_sum(1).astype(BF16)

    for d in CHIPS:
        arrive(("a", *d))
        to_sibling(*d)
    arrive(("o", 0, 0))
    for d in CHIPS:
        arrive(("o", *d))
    fgrad_out[...] = full[0:9]

    for n in range(1, 16):
        reduce_copy(n, x, 0).wait_send()
    for copy in sends:
        copy.wait_send()
    assert not pending and len(sends) <= NSEM


def write_out(maps, igrad, fgrad, maps_out, igrad_out, fgrad_out, sem):
    copies = [
        pltpu.make_async_copy(fgrad, fgrad_out, sem.at[2]),
        pltpu.make_async_copy(maps, maps_out, sem.at[0]),
        pltpu.make_async_copy(igrad, igrad_out, sem.at[1]),
    ]
    for copy in copies:
        copy.start()
    for copy in copies:
        copy.wait()


def per_device(features, filters, cotangent):
    vmem = pl.BlockSpec(memory_space=pltpu.VMEM)
    hbm = pl.BlockSpec(memory_space=pltpu.HBM)
    dma = pltpu.SemaphoreType.DMA
    outs = (
        jax.ShapeDtypeStruct((1, 32, CELLS), BF16),
        jax.ShapeDtypeStruct((1, 32, CELLS), BF16),
        jax.ShapeDtypeStruct((9, 32, 512), F32),
    )
    features, filters, cotangent = (
        pltpu.with_memory_space_constraint(v, pltpu.HBM) for v in (features, filters, cotangent))
    results = pl.pallas_call(
        kernel,
        out_shape=outs,
        in_specs=[hbm] * 3,
        out_specs=(vmem,) * 3,
        scratch_shapes=[
            pltpu.VMEM((9, 32, 512), BF16),
            pltpu.VMEM((512, CELLS), BF16),
            pltpu.VMEM((512, CELLS), BF16),
            pltpu.VMEM((16, 32, 384), BF16),
            pltpu.VMEM((16, 32, 384), BF16),
            pltpu.VMEM((288, CELLS), BF16),
            pltpu.VMEM((288, CELLS), F32),
            pltpu.VMEM((10, 32, 512), F32),
            pltpu.VMEM((5, 32, 512), F32),
            pltpu.VMEM((5, 32, 512), F32),
            pltpu.VMEM((16, 5, 8, 128), F32),
            pltpu.VMEM((5, 8, 128), F32),
            pltpu.VMEM((10, 32, 512), F32),
            dma((3,)), dma((NSEM,)), dma((NSEM,)), dma((16,)), dma((16,)),
        ],
        compiler_params=pltpu.CompilerParams(
            collective_id=0, has_side_effects=True, vmem_limit_bytes=48 * 1024 * 1024),
        cost_estimate=pl.CostEstimate(flops=906_000_000, bytes_accessed=1_200_000, transcendentals=0),
        name="conv",
    )(features, filters, cotangent)
    return tuple(pl.pallas_call(
        write_out,
        out_shape=outs,
        in_specs=[pl.BlockSpec(memory_space=pl.ANY)] * 3,
        out_specs=(hbm,) * 3,
        compiler_params=pltpu.CompilerParams(vmem_limit_bytes=1024 * 1024),
        scratch_shapes=[dma((3,))],
        name="write_out",
    )(*results))


def solution(mesh):
    return jax.shard_map(
        per_device,
        mesh=mesh,
        in_specs=(P("rep", "chan", None), P(None, "chan", None), P("rep", "chan", None)),
        out_specs=(P("rep", "chan", None), P("rep", "chan", None), P(None, "chan", None)),
        check_vma=False,
    )
```

```python
import jax
import jax.numpy as jnp
from jax import lax
from jax.experimental import pallas as pl
from jax.experimental.pallas import tpu as pltpu
from jax.sharding import PartitionSpec as P

MESH = pl.DeviceIdType.MESH
F32 = jnp.float32
BF16 = jnp.bfloat16

CELLS = 1024
OFFSETS = [(a, b) for a in (-1, 0, 1) for b in (-1, 0, 1)]
CHIPS = sorted([(dx, dh) for dx in range(4) for dh in range(4) if (dx, dh) != (0, 0)], key=lambda d: -(d[0] % 2 + 2 * (d[0] == 2) + 2 * (d[1] % 2) + 4 * (d[1] == 2)))
PEERS = [(dy, dz) for dy in range(2) for dz in range(8) if (dy, dz) != (0, 0)]
NSEM = 96


def coords():
    rep = lax.axis_index("rep")
    chan = lax.axis_index("chan")
    return rep // 8, (rep // 2) % 4, rep % 2, chan // 8, chan % 8


def keep_mask(a, b):
    p = lax.broadcasted_iota(jnp.int32, (32, CELLS), 1)
    row = p // 64 + a
    col = p % 64 + b
    return (row >= 0) & (row < 16) & (col >= 0) & (col < 64)


def moved(value, a, b):
    step = 64 * a + b
    if step == 0:
        return value
    return jnp.where(keep_mask(a, b), pltpu.roll(value, (-step) % CELLS, 1), 0.0)


def kernel(feat_in, filt_in, cot_in, maps_out, igrad_out, fgrad_out,
           filt, c_all, f_all, w_all, w_send, taps, prod, grad, pair, half, slots, mine, full,
           in_sem, ss, rs, r_ss, r_rs):
    x, h, core, yl, z = coords()
    rep = lax.axis_index("rep")
    chan = lax.axis_index("chan")

    def chan_of(dy, dz):
        return ((yl + dy) % 2) * 8 + (z + dz + 8) % 8

    def chan_dev(dy, dz):
        return (rep, chan_of(dy, dz))

    def chip_dev(dx, dh):
        return ((((x + dx) % 4) * 4 + (h + dh) % 4) * 2 + core, chan)

    sibling = ((x * 4 + h) * 2 + 1 - core, chan)

    def rows(dy, dz):
        return pl.ds(pl.multiple_of(chan_of(dy, dz) * 32, 32), 32)

    barrier = pltpu.get_barrier_semaphore()
    for dev in [chan_dev(*d) for d in PEERS] + [chip_dev(*d) for d in CHIPS] + [sibling]:
        pl.semaphore_signal(barrier, inc=1, device_id=dev, device_id_type=MESH)

    loads = [
        pltpu.make_async_copy(cot_in.at[0], c_all.at[rows(0, 0)], in_sem.at[0]),
        pltpu.make_async_copy(feat_in.at[0], f_all.at[rows(0, 0)], in_sem.at[1]),
        pltpu.make_async_copy(filt_in, filt, in_sem.at[2]),
    ]
    for load in loads:
        load.start()
    for load in loads:
        load.wait()
    pl.semaphore_wait(barrier, len(PEERS) + len(CHIPS) + 1)

    sends, pending = [], {}

    def start(key, src, dst, arrival, dev):
        n = len(sends)
        copy = pltpu.make_async_remote_copy(
            src_ref=src, dst_ref=dst, send_sem=ss.at[n], recv_sem=rs.at[n], device_id=dev, device_id_type=MESH)
        copy.start()
        sends.append(copy)
        pending[key] = pltpu.make_async_remote_copy(
            src_ref=arrival, dst_ref=arrival, send_sem=ss.at[n], recv_sem=rs.at[n], device_id=dev, device_id_type=MESH)

    def arrive(key):
        pending.pop(key).wait_recv()

    def pass_on(name, buf, dy, dz, hy, hz, part=0):
        cols = [pl.ds(0, CELLS), pl.ds(0, CELLS // 2), pl.ds(CELLS // 2, CELLS // 2)][part]
        place = buf.at[rows(dy, dz), cols]
        start((name, (dy + hy) % 2, dz - hz, part), place, place, buf.at[rows(dy + hy, dz - hz), cols], chan_dev(hy, hz))

    pass_on("c", c_all, 0, 0, 1, 0)
    for dz in (2, -2, 1, -1):
        pass_on("c", c_all, 0, 0, 0, dz)
    pass_on("f", f_all, 0, 0, 1, 0)

    value = f_all[rows(0, 0), :].astype(F32)
    for t, (a, b) in enumerate(OFFSETS):
        taps[t * 32:(t + 1) * 32, :] = moved(value, a, b).astype(BF16)
    grad[9] = jnp.zeros((32, 512), F32)

    for dz, side in ((2, 1), (-2, 2)):
        arrive(("c", 0, dz, 0))
        hop = -1 if dz > 0 else 1
        pass_on("c", c_all, 0, dz, 0, hop)
        pass_on("c", c_all, 0, dz, 0, 2 * hop, side)
    pass_on("c", c_all, 0, 2, 1, 0)
    pass_on("c", c_all, 0, -2, 1, 0)
    for dz in (1, -1):
        arrive(("c", 0, dz, 0))
        pass_on("c", c_all, 0, dz, 1, 0)

    arrive(("f", 1, 0, 0))
    for dz in (1, -1, 2, -2, 3, -3):
        for dy in (0, 1):
            pass_on("f", f_all, dy, 0, 0, dz)

    for d in range(16):
        parts = [filt[t, :, d * 32:(d + 1) * 32].astype(F32) for t in range(9)]
        parts.append(jnp.zeros((32, 96), F32))
        w_send[d] = jnp.concatenate(parts, axis=1).astype(BF16)
    my_rows = pl.ds(pl.multiple_of(core * 16, 16), 16)
    their_rows = pl.ds(pl.multiple_of((1 - core) * 16, 16), 16)
    w_all[chan] = w_send[chan]

    for dz in (3, -3):
        arrive(("c", 0, dz, 0))
        pass_on("c", c_all, 0, dz, 1, 0)
    arrive(("c", 0, 4, 1))
    pass_on("c", c_all, 0, 4, 1, 0, 1)
    arrive(("c", 0, -4, 2))
    pass_on("c", c_all, 0, -4, 1, 0, 2)

    my_taps = pl.ds(core * 5, 5)
    other_taps = pl.ds((1 - core) * 5, 5)

    def place(lane_tile, dh):
        return pl.ds(pl.multiple_of(((h + dh) % 4) * 8, 8), 8), pl.ds(pl.multiple_of(lane_tile * 128, 128), 128)

    def column(dy):
        return pl.ds(pl.multiple_of(((yl + dy) % 2) * 256, 256), 256)

    def grad_column(dy):
        side = column(dy)
        tile = lax.dot_general(taps[...], c_all[side, :], (((1,), (1,)), ((), ())), preferred_element_type=F32)
        grad[0:9, :, side] = tile.reshape(9, 32, 256)
        start(("pair", dy), grad.at[other_taps, :, side], pair.at[:, :, side], pair.at[:, :, side], sibling)

    def reduce_copy(n, lane_tile, dh):
        r, c = place(lane_tile, dh)
        return pltpu.make_async_remote_copy(
            src_ref=half.at[:, r, c], dst_ref=slots.at[n], send_sem=r_ss.at[n], recv_sem=r_rs.at[n],
            device_id=((lane_tile * 4 + (h + dh) % 4) * 2 + core, chan), device_id_type=MESH)

    def reduce_column(dy):
        side = column(dy)
        arrive(("pair", dy))
        half[:, :, side] = grad[my_taps, :, side] + pair[:, :, side]
        for k in (0, 1):
            lane_tile = ((yl + dy) % 2) * 2 + k
            for dh in (2, 1, 3, 0):
                n = ((lane_tile - x + 4) % 4) * 4 + dh

                @pl.when(n != 0)
                def _():
                    reduce_copy(n, lane_tile, dh).start()

    grad_column(0)
    reduce_column(0)

    for dz in (0, 1, -1, 2, -2, 3, -3):
        arrive(("c", 1, dz, 0))
    arrive(("c", 1, 4, 1))
    arrive(("c", 1, -4, 2))
    grad_column(1)
    reduce_column(1)

    for n, (dy, dz) in enumerate(PEERS):
        start(("w", n), w_send.at[chan_of(dy, dz), my_rows], w_all.at[chan, my_rows],
              w_all.at[chan_of(dy, -dz), my_rows], chan_dev(dy, dz))


    def tap_products(lhs, rhs):
        def tile(n, _):
            c = pl.ds(pl.multiple_of(n * 256, 256), 256)
            prod[:, c] = lhs(rhs[:, c])
            return 0

        lax.fori_loop(0, 4, tile, 0)

    def tap_sum(sign):
        total = prod[4 * 32:5 * 32, :]
        for t, (a, b) in enumerate(OFFSETS):
            if t != 4:
                total = total + moved(prod[t * 32:(t + 1) * 32, :], sign * a, sign * b)
        return total

    tap_products(lambda v: jnp.dot(filt[...].reshape(288, 512), v, preferred_element_type=F32), c_all)
    igrad_out[0] = tap_sum(-1).astype(BF16)

    r0, c0 = place(x, 0)
    for n in range(1, 16):
        reduce_copy(n, x, 0).wait_recv()
    total = half[:, r0, c0]
    for n in range(1, 16):
        total = total + slots[n]
    total = total * (1.0 / 32.0)
    mine[...] = total
    full[my_taps, r0, c0] = total
    for dx, dh in CHIPS:
        r, c = place((x + 4 - dx) % 4, 4 - dh)
        start(("a", dx, dh), mine, full.at[my_taps, r0, c0], full.at[my_taps, r, c], chip_dev(dx, dh))

    def to_sibling(dx, dh):
        r, c = place((x + 4 - dx) % 4, 4 - dh)
        start(("o", dx, dh), full.at[my_taps, r, c], full.at[my_taps, r, c], full.at[other_taps, r, c], sibling)

    to_sibling(0, 0)

    for dy in (0, 1):
        arrive(("f", dy, 3, 0))
        pass_on("f", f_all, dy, 3, 0, -1, 1)
        arrive(("f", dy, -3, 0))
        pass_on("f", f_all, dy, -3, 0, 1, 2)

    for n, d in enumerate(PEERS):
        arrive(("w", n))
    start("wpair", w_all.at[:, my_rows], w_all.at[:, my_rows], w_all.at[:, their_rows], sibling)
    for d in CHIPS:
        arrive(("a", *d))
        to_sibling(*d)
    for dy in (0, 1):
        for dz in (1, -1, 2, -2):
            arrive(("f", dy, dz, 0))
        arrive(("f", dy, 4, 1))
        arrive(("f", dy, -4, 2))
    arrive("wpair")

    def forward(v):
        return lax.dot_general(w_all[...].reshape(512, 384)[:, :288], v, (((0,), (0,)), ((), ())),
                               preferred_element_type=F32)

    tap_products(forward, f_all)
    maps_out[0] = tap_sum(1).astype(BF16)

    arrive(("o", 0, 0))
    for d in CHIPS:
        arrive(("o", *d))
    fgrad_out[...] = full[0:9]

    for n in range(1, 16):
        reduce_copy(n, x, 0).wait_send()
    for copy in sends:
        copy.wait_send()
    assert not pending and len(sends) <= NSEM


def write_out(maps, igrad, fgrad, maps_out, igrad_out, fgrad_out, sem):
    copies = [
        pltpu.make_async_copy(fgrad, fgrad_out, sem.at[2]),
        pltpu.make_async_copy(maps, maps_out, sem.at[0]),
        pltpu.make_async_copy(igrad, igrad_out, sem.at[1]),
    ]
    for copy in copies:
        copy.start()
    for copy in copies:
        copy.wait()


def per_device(features, filters, cotangent):
    vmem = pl.BlockSpec(memory_space=pltpu.VMEM)
    hbm = pl.BlockSpec(memory_space=pltpu.HBM)
    dma = pltpu.SemaphoreType.DMA
    outs = (
        jax.ShapeDtypeStruct((1, 32, CELLS), BF16),
        jax.ShapeDtypeStruct((1, 32, CELLS), BF16),
        jax.ShapeDtypeStruct((9, 32, 512), F32),
    )
    features, filters, cotangent = (
        pltpu.with_memory_space_constraint(v, pltpu.HBM) for v in (features, filters, cotangent))
    results = pl.pallas_call(
        kernel,
        out_shape=outs,
        in_specs=[hbm] * 3,
        out_specs=(vmem,) * 3,
        scratch_shapes=[
            pltpu.VMEM((9, 32, 512), BF16),
            pltpu.VMEM((512, CELLS), BF16),
            pltpu.VMEM((512, CELLS), BF16),
            pltpu.VMEM((16, 32, 384), BF16),
            pltpu.VMEM((16, 32, 384), BF16),
            pltpu.VMEM((288, CELLS), BF16),
            pltpu.VMEM((288, CELLS), F32),
            pltpu.VMEM((10, 32, 512), F32),
            pltpu.VMEM((5, 32, 512), F32),
            pltpu.VMEM((5, 32, 512), F32),
            pltpu.VMEM((16, 5, 8, 128), F32),
            pltpu.VMEM((5, 8, 128), F32),
            pltpu.VMEM((10, 32, 512), F32),
            dma((3,)), dma((NSEM,)), dma((NSEM,)), dma((16,)), dma((16,)),
        ],
        compiler_params=pltpu.CompilerParams(
            collective_id=0, has_side_effects=True, vmem_limit_bytes=48 * 1024 * 1024),
        cost_estimate=pl.CostEstimate(flops=906_000_000, bytes_accessed=1_200_000, transcendentals=0),
        name="conv",
    )(features, filters, cotangent)
    return tuple(pl.pallas_call(
        write_out,
        out_shape=outs,
        in_specs=[pl.BlockSpec(memory_space=pl.ANY)] * 3,
        out_specs=(hbm,) * 3,
        compiler_params=pltpu.CompilerParams(vmem_limit_bytes=1024 * 1024),
        scratch_shapes=[dma((3,))],
        name="write_out",
    )(*results))


def solution(mesh):
    return jax.shard_map(
        per_device,
        mesh=mesh,
        in_specs=(P("rep", "chan", None), P(None, "chan", None), P("rep", "chan", None)),
        out_specs=(P("rep", "chan", None), P("rep", "chan", None), P(None, "chan", None)),
        check_vma=False,
    )
```

```python
import jax
import jax.numpy as jnp
from jax import lax
from jax.experimental import pallas as pl
from jax.experimental.pallas import tpu as pltpu
from jax.sharding import PartitionSpec as P

MESH = pl.DeviceIdType.MESH
F32 = jnp.float32
BF16 = jnp.bfloat16

CELLS = 1024
OFFSETS = [(a, b) for a in (-1, 0, 1) for b in (-1, 0, 1)]
CHIPS = sorted([(dx, dh) for dx in range(4) for dh in range(4) if (dx, dh) != (0, 0)], key=lambda d: -(d[0] % 2 + 2 * (d[0] == 2) + 2 * (d[1] % 2) + 4 * (d[1] == 2)))
PEERS = [(dy, dz) for dy in range(2) for dz in range(8) if (dy, dz) != (0, 0)]
NSEM = 96


def coords():
    rep = lax.axis_index("rep")
    chan = lax.axis_index("chan")
    return rep // 8, (rep // 2) % 4, rep % 2, chan // 8, chan % 8


def keep_mask(a, b):
    p = lax.broadcasted_iota(jnp.int32, (32, CELLS), 1)
    row = p // 64 + a
    col = p % 64 + b
    return (row >= 0) & (row < 16) & (col >= 0) & (col < 64)


def moved(value, a, b):
    step = 64 * a + b
    if step == 0:
        return value
    return jnp.where(keep_mask(a, b), pltpu.roll(value, (-step) % CELLS, 1), 0.0)


def kernel(feat_in, filt_in, cot_in, maps_out, igrad_out, full,
           filt, c_all, f_all, w_all, w_send, taps, prod, grad, pair, half, slots, mine,
           in_sem, ss, rs, r_ss, r_rs):
    x, h, core, yl, z = coords()
    rep = lax.axis_index("rep")
    chan = lax.axis_index("chan")

    def chan_of(dy, dz):
        return ((yl + dy) % 2) * 8 + (z + dz + 8) % 8

    def chan_dev(dy, dz):
        return (rep, chan_of(dy, dz))

    def chip_dev(dx, dh):
        return ((((x + dx) % 4) * 4 + (h + dh) % 4) * 2 + core, chan)

    sibling = ((x * 4 + h) * 2 + 1 - core, chan)

    def rows(dy, dz):
        return pl.ds(pl.multiple_of(chan_of(dy, dz) * 32, 32), 32)

    loads = [
        pltpu.make_async_copy(cot_in.at[0], c_all.at[rows(0, 0)], in_sem.at[0]),
        pltpu.make_async_copy(feat_in.at[0], f_all.at[rows(0, 0)], in_sem.at[1]),
        pltpu.make_async_copy(filt_in, filt, in_sem.at[2]),
    ]
    for load in loads:
        load.start()

    barrier = pltpu.get_barrier_semaphore()
    for dev in [chip_dev(*d) for d in CHIPS] + [chan_dev(*d) for d in PEERS] + [sibling]:
        pl.semaphore_signal(barrier, inc=1, device_id=dev, device_id_type=MESH)

    loads[0].wait()
    pl.semaphore_wait(barrier, len(PEERS) + len(CHIPS) + 1)

    sends, pending = [], {}

    def start(key, src, dst, arrival, dev):
        n = len(sends)
        copy = pltpu.make_async_remote_copy(
            src_ref=src, dst_ref=dst, send_sem=ss.at[n], recv_sem=rs.at[n], device_id=dev, device_id_type=MESH)
        copy.start()
        sends.append(copy)
        pending[key] = pltpu.make_async_remote_copy(
            src_ref=arrival, dst_ref=arrival, send_sem=ss.at[n], recv_sem=rs.at[n], device_id=dev, device_id_type=MESH)

    def arrive(key):
        pending.pop(key).wait_recv()

    def pass_on(name, buf, dy, dz, hy, hz, part=0):
        cols = [pl.ds(0, CELLS), pl.ds(0, CELLS // 2), pl.ds(CELLS // 2, CELLS // 2)][part]
        place = buf.at[rows(dy, dz), cols]
        start((name, (dy + hy) % 2, dz - hz, part), place, place, buf.at[rows(dy + hy, dz - hz), cols], chan_dev(hy, hz))

    pass_on("c", c_all, 0, 0, 1, 0)
    for dz in (2, -2, 1, -1):
        pass_on("c", c_all, 0, 0, 0, dz)
    loads[1].wait()
    pass_on("f", f_all, 0, 0, 1, 0)
    loads[2].wait()

    value = f_all[rows(0, 0), :].astype(F32)
    for t, (a, b) in enumerate(OFFSETS):
        taps[t * 32:(t + 1) * 32, :] = moved(value, a, b).astype(BF16)
    grad[9] = jnp.zeros((32, 512), F32)

    for dz, side in ((2, 1), (-2, 2)):
        arrive(("c", 0, dz, 0))
        hop = -1 if dz > 0 else 1
        pass_on("c", c_all, 0, dz, 0, hop)
        pass_on("c", c_all, 0, dz, 0, 2 * hop, side)
    pass_on("c", c_all, 0, 2, 1, 0)
    pass_on("c", c_all, 0, -2, 1, 0)
    for dz in (1, -1):
        arrive(("c", 0, dz, 0))
        pass_on("c", c_all, 0, dz, 1, 0)

    arrive(("f", 1, 0, 0))
    for dz in (1, -1, 2, -2, 3, -3):
        for dy in (0, 1):
            pass_on("f", f_all, dy, 0, 0, dz)

    for d in range(16):
        parts = [filt[t, :, d * 32:(d + 1) * 32].astype(F32) for t in range(9)]
        parts.append(jnp.zeros((32, 96), F32))
        w_send[d] = jnp.concatenate(parts, axis=1).astype(BF16)
    my_rows = pl.ds(pl.multiple_of(core * 16, 16), 16)
    their_rows = pl.ds(pl.multiple_of((1 - core) * 16, 16), 16)
    w_all[chan] = w_send[chan]

    for dz in (3, -3):
        arrive(("c", 0, dz, 0))
        pass_on("c", c_all, 0, dz, 1, 0)
    arrive(("c", 0, 4, 1))
    pass_on("c", c_all, 0, 4, 1, 0, 1)
    arrive(("c", 0, -4, 2))
    pass_on("c", c_all, 0, -4, 1, 0, 2)

    my_taps = pl.ds(core * 5, 5)
    other_taps = pl.ds((1 - core) * 5, 5)

    def place(lane_tile, dh):
        return pl.ds(pl.multiple_of(((h + dh) % 4) * 8, 8), 8), pl.ds(pl.multiple_of(lane_tile * 128, 128), 128)

    def column(dy):
        return pl.ds(pl.multiple_of(((yl + dy) % 2) * 256, 256), 256)

    def grad_column(dy):
        side = column(dy)
        tile = lax.dot_general(taps[...], c_all[side, :], (((1,), (1,)), ((), ())), preferred_element_type=F32)
        grad[0:9, :, side] = tile.reshape(9, 32, 256)
        start(("pair", dy), grad.at[other_taps, :, side], pair.at[:, :, side], pair.at[:, :, side], sibling)

    def reduce_copy(n, lane_tile, dh):
        r, c = place(lane_tile, dh)
        return pltpu.make_async_remote_copy(
            src_ref=half.at[:, r, c], dst_ref=slots.at[n], send_sem=r_ss.at[n], recv_sem=r_rs.at[n],
            device_id=((lane_tile * 4 + (h + dh) % 4) * 2 + core, chan), device_id_type=MESH)

    def reduce_column(dy):
        side = column(dy)
        arrive(("pair", dy))
        half[:, :, side] = grad[my_taps, :, side] + pair[:, :, side]
        for k in (0, 1):
            lane_tile = ((yl + dy) % 2) * 2 + k
            for dh in (2, 1, 3, 0):
                n = ((lane_tile - x + 4) % 4) * 4 + dh

                @pl.when(n != 0)
                def _():
                    reduce_copy(n, lane_tile, dh).start()

    grad_column(0)
    reduce_column(0)

    for dz in (0, 1, -1, 2, -2, 3, -3):
        arrive(("c", 1, dz, 0))
    arrive(("c", 1, 4, 1))
    arrive(("c", 1, -4, 2))
    grad_column(1)
    reduce_column(1)

    for n, (dy, dz) in enumerate(PEERS):
        start(("w", n), w_send.at[chan_of(dy, dz), my_rows], w_all.at[chan, my_rows],
              w_all.at[chan_of(dy, -dz), my_rows], chan_dev(dy, dz))


    def tap_products(lhs, rhs):
        def tile(n, _):
            c = pl.ds(pl.multiple_of(n * 256, 256), 256)
            prod[:, c] = lhs(rhs[:, c])
            return 0

        lax.fori_loop(0, 4, tile, 0)

    def tap_sum(sign):
        total = prod[4 * 32:5 * 32, :]
        for t, (a, b) in enumerate(OFFSETS):
            if t != 4:
                total = total + moved(prod[t * 32:(t + 1) * 32, :], sign * a, sign * b)
        return total

    tap_products(lambda v: jnp.dot(filt[...].reshape(288, 512), v, preferred_element_type=F32), c_all)
    igrad_out[0] = tap_sum(-1).astype(BF16)

    r0, c0 = place(x, 0)
    for n in range(1, 16):
        reduce_copy(n, x, 0).wait_recv()
    total = half[:, r0, c0]
    for n in range(1, 16):
        total = total + slots[n]
    total = total * (1.0 / 32.0)
    mine[...] = total
    full[my_taps, r0, c0] = total
    for dx, dh in CHIPS:
        r, c = place((x + 4 - dx) % 4, 4 - dh)
        start(("a", dx, dh), mine, full.at[my_taps, r0, c0], full.at[my_taps, r, c], chip_dev(dx, dh))

    def to_sibling(dx, dh):
        r, c = place((x + 4 - dx) % 4, 4 - dh)
        start(("o", dx, dh), full.at[my_taps, r, c], full.at[my_taps, r, c], full.at[other_taps, r, c], sibling)

    to_sibling(0, 0)

    for dy in (0, 1):
        arrive(("f", dy, 3, 0))
        pass_on("f", f_all, dy, 3, 0, -1, 1)
        arrive(("f", dy, -3, 0))
        pass_on("f", f_all, dy, -3, 0, 1, 2)

    for n, d in enumerate(PEERS):
        arrive(("w", n))
    start("wpair", w_all.at[:, my_rows], w_all.at[:, my_rows], w_all.at[:, their_rows], sibling)
    for d in CHIPS:
        arrive(("a", *d))
        to_sibling(*d)
    for dy in (0, 1):
        for dz in (1, -1, 2, -2):
            arrive(("f", dy, dz, 0))
        arrive(("f", dy, 4, 1))
        arrive(("f", dy, -4, 2))
    arrive("wpair")

    def forward(v):
        return lax.dot_general(w_all[...].reshape(512, 384)[:, :288], v, (((0,), (0,)), ((), ())),
                               preferred_element_type=F32)

    tap_products(forward, f_all)
    maps_out[0] = tap_sum(1).astype(BF16)

    arrive(("o", 0, 0))
    for d in CHIPS:
        arrive(("o", *d))

    for n in range(1, 16):
        reduce_copy(n, x, 0).wait_send()
    for copy in sends:
        copy.wait_send()
    assert not pending and len(sends) <= NSEM


def write_out(maps, igrad, fgrad, maps_out, igrad_out, fgrad_out, sem):
    copies = [
        pltpu.make_async_copy(fgrad.at[0:9], fgrad_out, sem.at[2]),
        pltpu.make_async_copy(maps, maps_out, sem.at[0]),
        pltpu.make_async_copy(igrad, igrad_out, sem.at[1]),
    ]
    for copy in copies:
        copy.start()
    for copy in copies:
        copy.wait()


def per_device(features, filters, cotangent):
    vmem = pl.BlockSpec(memory_space=pltpu.VMEM)
    hbm = pl.BlockSpec(memory_space=pltpu.HBM)
    dma = pltpu.SemaphoreType.DMA
    outs = (
        jax.ShapeDtypeStruct((1, 32, CELLS), BF16),
        jax.ShapeDtypeStruct((1, 32, CELLS), BF16),
        jax.ShapeDtypeStruct((9, 32, 512), F32),
    )
    features, filters, cotangent = (
        pltpu.with_memory_space_constraint(v, pltpu.HBM) for v in (features, filters, cotangent))
    results = pl.pallas_call(
        kernel,
        out_shape=outs[:2] + (jax.ShapeDtypeStruct((10, 32, 512), F32),),
        in_specs=[hbm] * 3,
        out_specs=(vmem,) * 3,
        scratch_shapes=[
            pltpu.VMEM((9, 32, 512), BF16),
            pltpu.VMEM((512, CELLS), BF16),
            pltpu.VMEM((512, CELLS), BF16),
            pltpu.VMEM((16, 32, 384), BF16),
            pltpu.VMEM((16, 32, 384), BF16),
            pltpu.VMEM((288, CELLS), BF16),
            pltpu.VMEM((288, CELLS), F32),
            pltpu.VMEM((10, 32, 512), F32),
            pltpu.VMEM((5, 32, 512), F32),
            pltpu.VMEM((5, 32, 512), F32),
            pltpu.VMEM((16, 5, 8, 128), F32),
            pltpu.VMEM((5, 8, 128), F32),
            dma((3,)), dma((NSEM,)), dma((NSEM,)), dma((16,)), dma((16,)),
        ],
        compiler_params=pltpu.CompilerParams(
            collective_id=0, has_side_effects=True, vmem_limit_bytes=48 * 1024 * 1024),
        cost_estimate=pl.CostEstimate(flops=906_000_000, bytes_accessed=1_200_000, transcendentals=0),
        name="conv",
    )(features, filters, cotangent)
    return tuple(pl.pallas_call(
        write_out,
        out_shape=outs,
        in_specs=[pl.BlockSpec(memory_space=pl.ANY)] * 3,
        out_specs=(hbm,) * 3,
        compiler_params=pltpu.CompilerParams(vmem_limit_bytes=1024 * 1024),
        scratch_shapes=[dma((3,))],
        name="write_out",
    )(*results))


def solution(mesh):
    return jax.shard_map(
        per_device,
        mesh=mesh,
        in_specs=(P("rep", "chan", None), P(None, "chan", None), P("rep", "chan", None)),
        out_specs=(P("rep", "chan", None), P("rep", "chan", None), P(None, "chan", None)),
        check_vma=False,
    )
```
